32 devices in a mesh: lat: 4 (over y, x), lon: 8 (over z, core).
Axes of the slice: x: 2, y: 2, z: 4, core: 2. Of those that a mesh axis runs over, the one named last changes fastest.
Arguments:
- queries: bfloat16 [8, 32, 32, 640], P(None, 'lat', 'lon'), may hold values from -12 to 12
- key_vectors: bfloat16 [8, 32, 32, 640], P(None, 'lat', 'lon'), may hold values from -12 to 12
- values: bfloat16 [8, 32, 32, 640], P(None, 'lat', 'lon'), may hold values from -6 to 6
- upstream: bfloat16 [8, 32, 32, 640], P(None, 'lat', 'lon'), may hold values from -6 to 6
Outputs:
- attended: bfloat16 [8, 32, 32, 640], P(None, 'lat', 'lon')
- grad_queries: bfloat16 [8, 32, 32, 640], P(None, 'lat', 'lon')
- grad_keys: bfloat16 [8, 32, 32, 640], P(None, 'lat', 'lon')
- grad_values: bfloat16 [8, 32, 32, 640], P(None, 'lat', 'lon')
The draws below stay inside these ranges and needn't reach their ends.
All inputs are finite; a program needn't handle non-finite values.
Results may differ from the reference program's by a relative error of at most 0.0044.
The reference program's roundings to bfloat16 on the way count: a program that leaves them out, or rounds other values in their place, can miss the bound.
Values may be sent and summed in bfloat16 or wider, within the bound.
A program may use at most 64 MiB of HBM per device.

```python
import jax
import jax.numpy as jnp
from jax import lax

BATCH = 8
HEADS = 10
HEAD_DIM = 64
FEAT = 640
LATS = 32
LONS = 32


def drawn_field(key, salt):
    noise = jax.random.normal(jax.random.fold_in(key, salt), (BATCH, LATS, LONS, HEADS * HEAD_DIM), jnp.float32)
    return jnp.clip(noise, -12.0, 12.0).astype(jnp.bfloat16)


def draw_queries(key, part):
    return drawn_field(key, 11)


def draw_key_vectors(key, part):
    return drawn_field(key, 23)


def shard_levels(key, extent, shards, smallest, largest):
    level = 1.0
    for position, parts in shards:
        draws = jax.random.uniform(jax.random.fold_in(jax.random.fold_in(key, 6), position), (parts,), jnp.float32, smallest / len(shards), largest / len(shards))
        level = level * jnp.repeat(jnp.exp(draws), extent[position] // parts).reshape((-1,) + (1,) * (len(extent) - 1 - position))
    return level


def normal_values(key, shape, scale, limit, cuts=(), held_as=jnp.bfloat16):
    gain = shard_levels(key, shape, cuts, -0.22, 0.18) if cuts else 1.0
    entries = jax.random.normal(key, shape, jnp.float32) * scale * gain
    return jnp.minimum(jnp.maximum(entries, -limit), limit).astype(held_as)


def setup_inputs(seed: int = 0) -> dict:
    streams_of = jax.random.split(jax.random.key(seed), 5)
    queries = draw_queries(jax.random.fold_in(streams_of[4], 71), 0)
    key_vectors = draw_key_vectors(jax.random.fold_in(streams_of[4], 71), 0)
    values = normal_values(streams_of[2], (BATCH, LATS, LONS, FEAT), 1.0, 6.0, ((1, 4), (2, 8)))
    upstream = normal_values(streams_of[3], (BATCH, LATS, LONS, FEAT), 1.0, 6.0, ((1, 4), (2, 8)))
    return dict(queries=queries, key_vectors=key_vectors, values=values, upstream=upstream)


def axial_lines(queries, key_vectors, values, upstream):
    count = queries.shape[0]
    length = queries.shape[1]
    heads = queries.shape[2] // HEAD_DIM
    query_heads = queries.astype(jnp.float32).reshape(count, length, heads, HEAD_DIM)
    key_heads = key_vectors.astype(jnp.float32).reshape(count, length, heads, HEAD_DIM)
    value_heads = values.astype(jnp.float32).reshape(count, length, heads, HEAD_DIM)
    grad_heads = upstream.astype(jnp.float32).reshape(count, length, heads, HEAD_DIM)
    score_scale = HEAD_DIM ** -0.5
    scores = jnp.einsum("nqhd,nkhd->nhqk", query_heads, key_heads) * score_scale
    probs = jax.nn.softmax(scores, axis=-1)
    rounded = lax.optimization_barrier(probs.astype(jnp.bfloat16)).astype(jnp.float32)
    output = jnp.einsum("nhqk,nkhd->nqhd", rounded, value_heads)
    grad_probs = jnp.einsum("nqhd,nkhd->nhqk", grad_heads, value_heads)
    row_delta = jnp.sum(probs * grad_probs, axis=-1, keepdims=True)
    grad_scores = probs * (grad_probs - row_delta)
    grad_scores = lax.optimization_barrier(grad_scores.astype(jnp.bfloat16)).astype(jnp.float32)
    grad_value_heads = jnp.einsum("nhqk,nqhd->nkhd", rounded, grad_heads)
    grad_query_heads = jnp.einsum("nhqk,nkhd->nqhd", grad_scores, key_heads) * score_scale
    grad_key_heads = jnp.einsum("nhqk,nqhd->nkhd", grad_scores, query_heads) * score_scale
    results = (output, grad_query_heads, grad_key_heads, grad_value_heads)
    return tuple(item.reshape(count, length, heads * HEAD_DIM).astype(jnp.bfloat16) for item in results)


def one_sample(items):
    queries, key_vectors, values, upstream = items
    along_lon = axial_lines(queries, key_vectors, values, upstream)
    turned = tuple(item.transpose(1, 0, 2) for item in (queries, key_vectors, values, upstream))
    along_lat = tuple(item.transpose(1, 0, 2) for item in axial_lines(*turned))
    return tuple((first.astype(jnp.float32) + second.astype(jnp.float32)).astype(jnp.bfloat16) for first, second in zip(along_lat, along_lon))


def reference(queries, key_vectors, values, upstream):
    attended, grad_queries, grad_keys, grad_values = lax.map(one_sample, (queries, key_vectors, values, upstream))
    return (attended, grad_queries, grad_keys, grad_values)
```

```python
import functools

import jax
import jax.numpy as jnp
from jax import lax
from jax.experimental import pallas as pl
from jax.experimental.pallas import tpu as pltpu
from jax.sharding import PartitionSpec as P

HEAD_DIM = 64
LANES = 128
SUBROWS = 16
SCALE = HEAD_DIM ** (-0.5)
F32 = jnp.float32
BF16 = jnp.bfloat16


def contract(left, right, dims):
    return lax.dot_general(left, right, ((dims[:1], dims[1:]), ((), ())), preferred_element_type=F32)


def lines_block(q, k, v, g, same, low, high):
    tokens = q.shape[0]
    q2 = jnp.concatenate([q * low, q * high], axis=0)
    k2 = jnp.concatenate([k * low, k * high], axis=0)
    v2 = jnp.concatenate([v * low, v * high], axis=0)
    g2 = jnp.concatenate([g * low, g * high], axis=0)
    scores = contract(q, k2, (1, 1))
    gprobs = contract(g, v2, (1, 1))
    probs_b, gscores_b = [], []
    for head in range(2):
        cut = slice(head * tokens, (head + 1) * tokens)
        s = jnp.where(same, scores[:, cut] * SCALE, -1e30)
        e = jnp.exp(s - jnp.max(s, axis=1, keepdims=True))
        p = e / jnp.sum(e, axis=1, keepdims=True)
        d = gprobs[:, cut]
        delta = jnp.sum(p * d, axis=1, keepdims=True)
        probs_b.append(p.astype(BF16))
        gscores_b.append((p * (d - delta)).astype(BF16))
    out = contract(jnp.concatenate(probs_b, axis=1), v2, (1, 0))
    dq = contract(jnp.concatenate(gscores_b, axis=1), k2, (1, 0)) * SCALE
    dk = contract(jnp.concatenate(gscores_b, axis=0), q2, (0, 0)) * SCALE
    dv = contract(jnp.concatenate(probs_b, axis=0), g2, (0, 0))
    return out.astype(BF16), dq.astype(BF16), dk.astype(BF16), dv.astype(BF16)


def kernel(
    n_lat, n_lon, cols, x_ref, out_ref,
    in_lat, in_lon, res_lat, res_lon, ret_lat, ret_lon,
    s_in_lat, r_in_lat, s_in_lon, r_in_lon, s_out_lat, r_out_lat, s_out_lon, r_out_lon, own_sem,
):
    me_lat = lax.axis_index("lat")
    me_lon = lax.axis_index("lon")
    _, batch, tokens, feats = x_ref.shape
    per_lat = batch // n_lat
    parts = tokens // SUBROWS
    lat_peers = [(d, lax.rem(me_lat + d, n_lat)) for d in range(1, n_lat)]
    lon_order = sorted(range(1, n_lon), key=lambda d: abs(d - n_lon // 2))
    lon_peers = [(d, lax.rem(me_lon + d, n_lon)) for d in lon_order]

    barrier = pltpu.get_barrier_semaphore()
    for _, peer in lat_peers:
        pl.semaphore_signal(barrier, inc=1, device_id={"lat": peer}, device_id_type=pl.DeviceIdType.MESH)
    for _, peer in lon_peers:
        pl.semaphore_signal(barrier, inc=1, device_id={"lon": peer}, device_id_type=pl.DeviceIdType.MESH)
    pl.semaphore_wait(barrier, len(lat_peers) + len(lon_peers))

    def remote(src, dst, send, recv, target):
        return pltpu.make_async_remote_copy(
            src_ref=src, dst_ref=dst, send_sem=send, recv_sem=recv,
            device_id=target, device_id_type=pl.DeviceIdType.MESH,
        )

    def lat_in(i, d, peer):
        return remote(
            x_ref.at[:, peer * per_lat + i], in_lat.at[:, i, me_lat],
            s_in_lat.at[i, d], r_in_lat.at[i, d], {"lat": peer},
        )

    def lon_in(i, d, peer):
        return remote(
            x_ref.at[:, peer, pl.ds(i * SUBROWS, SUBROWS)], in_lon.at[:, i, me_lon],
            s_in_lon.at[i, d], r_in_lon.at[i, d], {"lon": peer},
        )

    def lat_out(i, d, peer):
        return remote(
            res_lat.at[:, i, peer], ret_lat.at[:, me_lat * per_lat + i],
            s_out_lat.at[i, d], r_out_lat.at[i, d], {"lat": peer},
        )

    def lon_out(i, d, peer):
        return remote(
            res_lon.at[:, i, peer], ret_lon.at[:, me_lon, pl.ds(i * SUBROWS, SUBROWS)],
            s_out_lon.at[i, d], r_out_lon.at[i, d], {"lon": peer},
        )

    for i in range(max(per_lat, parts)):
        if i < parts:
            for d, peer in lon_peers:
                lon_in(i, d, peer).start()
        if i < per_lat:
            for d, peer in lat_peers:
                lat_in(i, d, peer).start()

    owns = []
    for i in range(per_lat):
        owns.append(pltpu.make_async_copy(
            x_ref.at[:, me_lat * per_lat + i], in_lat.at[:, i, me_lat], own_sem.at[len(owns)]))
    for i in range(parts):
        owns.append(pltpu.make_async_copy(
            x_ref.at[:, me_lon, pl.ds(i * SUBROWS, SUBROWS)], in_lon.at[:, i, me_lon], own_sem.at[len(owns)]))
    for copy in owns:
        copy.start()

    lane = lax.broadcasted_iota(jnp.int32, (1, LANES), 1)
    low = (lane < HEAD_DIM).astype(F32).astype(BF16)
    high = (lane >= HEAD_DIM).astype(F32).astype(BF16)

    def attend(arrived, result, i, same):
        count, rows = arrived.shape[2], arrived.shape[3]

        def pair(h, carry):
            cut = pl.ds(pl.multiple_of(h * LANES, LANES), LANES)
            items = [arrived[a, i, :, :, cut].reshape(count * rows, LANES) for a in range(4)]
            for o, value in enumerate(lines_block(*items, same, low, high)):
                result[o, i, :, :, cut] = value.reshape(count, rows, LANES)
            return carry

        lax.fori_loop(0, feats // LANES, pair, 0)

    def same_line(size, line_of):
        a = line_of(lax.broadcasted_iota(jnp.int32, (size, size), 0))
        b = line_of(lax.broadcasted_iota(jnp.int32, (size, size), 1))
        return a == b

    same_lat = same_line(n_lat * tokens, lambda t: lax.rem(t, cols))
    same_lon = same_line(n_lon * SUBROWS, lambda t: lax.div(lax.rem(t, SUBROWS), cols))

    for i in range(per_lat):
        owns[i].wait()
        for d, peer in lat_peers:
            lat_in(i, d, peer).wait_recv()
        attend(in_lat, res_lat, i, same_lat)
        for d, peer in lat_peers:
            lat_out(i, d, peer).start()
        keep = pltpu.make_async_copy(
            res_lat.at[:, i, me_lat], ret_lat.at[:, me_lat * per_lat + i], own_sem.at[i])
        keep.start()
        owns[i] = keep
    for i in range(parts):
        owns[per_lat + i].wait()
        for d, peer in lon_peers:
            lon_in(i, d, peer).wait_recv()
        attend(in_lon, res_lon, i, same_lon)
        for d, peer in lon_peers:
            lon_out(i, d, peer).start()
        keep = pltpu.make_async_copy(
            res_lon.at[:, i, me_lon], ret_lon.at[:, me_lon, pl.ds(i * SUBROWS, SUBROWS)], own_sem.at[per_lat + i])
        keep.start()
        owns[per_lat + i] = keep

    for copy in owns:
        copy.wait()
    for i in range(per_lat):
        for d, peer in lat_peers:
            lat_out(i, d, peer).wait_recv()
    for i in range(parts):
        for d, peer in lon_peers:
            lon_out(i, d, peer).wait_recv()

        def add(b, carry):
            rows = pl.ds(i * SUBROWS, SUBROWS)
            for o in range(4):
                total = ret_lat[o, b, rows, :].astype(F32) + ret_lon[o, b, rows, :].astype(F32)
                out_ref[o, b, rows, :] = total.astype(BF16)
            return carry

        lax.fori_loop(0, batch, add, 0)

    for i in range(per_lat):
        for d, peer in lat_peers:
            lat_in(i, d, peer).wait_send()
            lat_out(i, d, peer).wait_send()
    for i in range(parts):
        for d, peer in lon_peers:
            lon_in(i, d, peer).wait_send()
            lon_out(i, d, peer).wait_send()


def by_kernel(n_lat, n_lon, queries, key_vectors, values, upstream):
    batch, rows, cols, feats = queries.shape
    tokens = rows * cols
    per_lat, parts = batch // n_lat, tokens // SUBROWS
    x = jnp.stack([queries, key_vectors, values, upstream]).reshape(4, batch, tokens, feats)
    lat_buf = pltpu.VMEM((4, per_lat, n_lat, tokens, feats), BF16)
    lon_buf = pltpu.VMEM((4, parts, n_lon, SUBROWS, feats), BF16)
    back_buf = pltpu.VMEM((4, batch, tokens, feats), BF16)
    lat_sem = pltpu.SemaphoreType.DMA((per_lat, n_lat))
    lon_sem = pltpu.SemaphoreType.DMA((parts, n_lon))
    y = pl.pallas_call(
        functools.partial(kernel, n_lat, n_lon, cols),
        out_shape=jax.ShapeDtypeStruct((4, batch, tokens, feats), BF16),
        in_specs=[pl.BlockSpec(memory_space=pltpu.VMEM)],
        out_specs=pl.BlockSpec(memory_space=pltpu.VMEM),
        scratch_shapes=[
            lat_buf, lon_buf, lat_buf, lon_buf, back_buf, back_buf,
            lat_sem, lat_sem, lon_sem, lon_sem, lat_sem, lat_sem, lon_sem, lon_sem,
            pltpu.SemaphoreType.DMA((per_lat + parts,)),
        ],
        compiler_params=pltpu.CompilerParams(
            collective_id=0, has_side_effects=True, vmem_limit_bytes=40 * 1024 * 1024
        ),
    )(x)
    return tuple(y[i].reshape(queries.shape) for i in range(4))


def split_heads(tensor):
    leading = tensor.shape[0] * tensor.shape[1]
    return tensor.reshape(leading, tensor.shape[2], tensor.shape[3] // HEAD_DIM, HEAD_DIM)


def lines_whole(items):
    q, k, v, g = (split_heads(item) for item in items)
    dot = functools.partial(jnp.einsum, preferred_element_type=F32)
    probs = jax.nn.softmax(dot("nqhd,nkhd->nhqk", q, k) * SCALE, axis=-1)
    rounded = probs.astype(BF16)
    gprobs = dot("nqhd,nkhd->nhqk", g, v)
    delta = jnp.sum(probs * gprobs, axis=-1, keepdims=True)
    gscores = (probs * (gprobs - delta)).astype(BF16)
    results = (
        dot("nhqk,nkhd->nqhd", rounded, v),
        dot("nhqk,nkhd->nqhd", gscores, k) * SCALE,
        dot("nhqk,nqhd->nkhd", gscores, q) * SCALE,
        dot("nhqk,nqhd->nkhd", rounded, g),
    )
    return tuple(item.astype(BF16).reshape(items[0].shape) for item in results)


def by_exchange(axis, groups, inputs):
    def there(item):
        lines = item.reshape((groups, item.shape[0] * item.shape[1] // groups) + item.shape[2:])
        return lax.all_to_all(lines, axis, split_axis=0, concat_axis=2, tiled=True)

    def back(item):
        item = lax.all_to_all(item, axis, split_axis=2, concat_axis=0, tiled=True)
        return item.reshape(inputs[0].shape)

    return tuple(back(item) for item in lines_whole(tuple(there(item) for item in inputs)))


def by_collectives(n_lat, n_lon, *inputs):
    lon = by_exchange("lon", n_lon, inputs)
    lat = by_exchange("lat", n_lat, tuple(item.transpose(0, 2, 1, 3) for item in inputs))
    return tuple(
        (a.transpose(0, 2, 1, 3).astype(F32) + b.astype(F32)).astype(BF16) for a, b in zip(lat, lon)
    )


def solution(mesh):
    n_lat, n_lon = mesh.shape["lat"], mesh.shape["lon"]

    def on_device(*inputs):
        batch, rows, cols, feats = inputs[0].shape
        fits = (
            batch % n_lat == 0 and batch == n_lon and n_lat > 1 and (rows * cols) % SUBROWS == 0
            and SUBROWS % cols == 0 and feats % LANES == 0 and 2 * HEAD_DIM == LANES
        )
        return (by_kernel if fits else by_collectives)(n_lat, n_lon, *inputs)

    spec = P(None, "lat", "lon", None)
    return jax.shard_map(on_device, mesh=mesh, in_specs=(spec,) * 4, out_specs=(spec,) * 4, check_vma=False)
```

```python
import functools

import jax
import jax.numpy as jnp
from jax import lax
from jax.experimental import pallas as pl
from jax.experimental.pallas import tpu as pltpu
from jax.sharding import PartitionSpec as P

HEAD_DIM = 64
LANES = 128
SUBROWS = 16
SCALE = HEAD_DIM ** (-0.5)
F32 = jnp.float32
BF16 = jnp.bfloat16


def contract(left, right, dims):
    return lax.dot_general(left, right, ((dims[:1], dims[1:]), ((), ())), preferred_element_type=F32)


def lines_block(q, k, v, g, same, low, high):
    tokens = q.shape[0]
    q2 = jnp.concatenate([q * low, q * high], axis=0)
    k2 = jnp.concatenate([k * low, k * high], axis=0)
    v2 = jnp.concatenate([v * low, v * high], axis=0)
    g2 = jnp.concatenate([g * low, g * high], axis=0)
    scores = contract(q, k2, (1, 1))
    gprobs = contract(g, v2, (1, 1))
    probs_b, gscores_b = [], []
    for head in range(2):
        cut = slice(head * tokens, (head + 1) * tokens)
        s = jnp.where(same, scores[:, cut] * SCALE, -1e30)
        e = jnp.exp(s - jnp.max(s, axis=1, keepdims=True))
        p = e / jnp.sum(e, axis=1, keepdims=True)
        d = gprobs[:, cut]
        delta = jnp.sum(p * d, axis=1, keepdims=True)
        probs_b.append(p.astype(BF16))
        gscores_b.append((p * (d - delta)).astype(BF16))
    out = contract(jnp.concatenate(probs_b, axis=1), v2, (1, 0))
    dq = contract(jnp.concatenate(gscores_b, axis=1), k2, (1, 0)) * SCALE
    dk = contract(jnp.concatenate(gscores_b, axis=0), q2, (0, 0)) * SCALE
    dv = contract(jnp.concatenate(probs_b, axis=0), g2, (0, 0))
    return out.astype(BF16), dq.astype(BF16), dk.astype(BF16), dv.astype(BF16)


def kernel(
    n_lat, n_lon, *refs,
):
    given, outs = refs[:4], refs[4:8]
    (
        near, x_ref, in_lat, in_lon, res_lat, res_lon, ret_lat, ret_lon,
    s_in_lat, r_in_lat, s_in_lon, r_in_lon, s_out_lat, r_out_lat, s_out_lon, r_out_lon, own_sem, load_sem,
    ) = refs[8:]
    me_lat = lax.axis_index("lat")
    me_lon = lax.axis_index("lon")
    _, batch, tokens, feats = x_ref.shape
    cols = near.shape[3]
    lines = SUBROWS // cols
    per_lat = batch // n_lat
    parts = tokens // SUBROWS
    lat_peers = [(d, lax.rem(me_lat + d, n_lat)) for d in range(1, n_lat)]
    lon_order = sorted(range(1, n_lon), key=lambda d: abs(d - n_lon // 2))
    lon_peers = [(d, lax.rem(me_lon + d, n_lon)) for d in lon_order]

    loads = [pltpu.make_async_copy(given[a], near.at[a], load_sem.at[a]) for a in range(4)]
    for copy in loads:
        copy.start()

    barrier = pltpu.get_barrier_semaphore()
    for _, peer in lat_peers:
        pl.semaphore_signal(barrier, inc=1, device_id={"lat": peer}, device_id_type=pl.DeviceIdType.MESH)
    for _, peer in lon_peers:
        pl.semaphore_signal(barrier, inc=1, device_id={"lon": peer}, device_id_type=pl.DeviceIdType.MESH)
    pl.semaphore_wait(barrier, len(lat_peers) + len(lon_peers))

    def remote(src, dst, send, recv, target):
        return pltpu.make_async_remote_copy(
            src_ref=src, dst_ref=dst, send_sem=send, recv_sem=recv,
            device_id=target, device_id_type=pl.DeviceIdType.MESH,
        )

    def lat_in(i, d, peer):
        return remote(
            x_ref.at[:, peer * per_lat + i], in_lat.at[:, i, me_lat],
            s_in_lat.at[i, d], r_in_lat.at[i, d], {"lat": peer},
        )

    def lon_in(i, d, peer):
        return remote(
            x_ref.at[:, peer, pl.ds(i * SUBROWS, SUBROWS)], in_lon.at[:, i, me_lon],
            s_in_lon.at[i, d], r_in_lon.at[i, d], {"lon": peer},
        )

    def lat_out(i, d, peer):
        return remote(
            res_lat.at[:, i, peer], ret_lat.at[:, me_lat * per_lat + i],
            s_out_lat.at[i, d], r_out_lat.at[i, d], {"lat": peer},
        )

    def lon_out(i, d, peer):
        return remote(
            res_lon.at[:, i, peer], ret_lon.at[:, me_lon, pl.ds(i * SUBROWS, SUBROWS)],
            s_out_lon.at[i, d], r_out_lon.at[i, d], {"lon": peer},
        )

    def lay(b, i):
        for a in range(4):
            for r in range(lines):
                x_ref[a, b, pl.ds(i * SUBROWS + r * cols, cols), :] = near[a, b, i * lines + r]

    for copy in loads:
        copy.wait()
    for d, peer in lon_peers:
        lay(peer, 0)
        lon_in(0, d, peer).start()
    lay(me_lon, 0)

    def lay_rest(b, carry):
        for i in range(1, parts):
            lay(b, i)
        return carry

    lax.fori_loop(0, batch, lay_rest, 0)
    for i in range(max(per_lat, parts)):
        if i < per_lat:
            for d, peer in lat_peers:
                lat_in(i, d, peer).start()
        if 0 < i < parts:
            for d, peer in lon_peers:
                lon_in(i, d, peer).start()

    owns = []
    for i in range(per_lat):
        owns.append(pltpu.make_async_copy(
            x_ref.at[:, me_lat * per_lat + i], in_lat.at[:, i, me_lat], own_sem.at[len(owns)]))
    for i in range(parts):
        owns.append(pltpu.make_async_copy(
            x_ref.at[:, me_lon, pl.ds(i * SUBROWS, SUBROWS)], in_lon.at[:, i, me_lon], own_sem.at[len(owns)]))
    for copy in owns:
        copy.start()

    lane = lax.broadcasted_iota(jnp.int32, (1, LANES), 1)
    low = (lane < HEAD_DIM).astype(F32).astype(BF16)
    high = (lane >= HEAD_DIM).astype(F32).astype(BF16)

    def attend(arrived, result, i, same):
        count, rows = arrived.shape[2], arrived.shape[3]

        def pair(h, carry):
            cut = pl.ds(pl.multiple_of(h * LANES, LANES), LANES)
            items = [arrived[a, i, :, :, cut].reshape(count * rows, LANES) for a in range(4)]
            for o, value in enumerate(lines_block(*items, same, low, high)):
                result[o, i, :, :, cut] = value.reshape(count, rows, LANES)
            return carry

        lax.fori_loop(0, feats // LANES, pair, 0)

    def same_line(size, line_of):
        a = line_of(lax.broadcasted_iota(jnp.int32, (size, size), 0))
        b = line_of(lax.broadcasted_iota(jnp.int32, (size, size), 1))
        return a == b

    same_lat = same_line(n_lat * tokens, lambda t: lax.rem(t, cols))
    same_lon = same_line(n_lon * SUBROWS, lambda t: lax.div(lax.rem(t, SUBROWS), cols))

    for i in range(per_lat):
        owns[i].wait()
        for d, peer in lat_peers:
            lat_in(i, d, peer).wait_recv()
        attend(in_lat, res_lat, i, same_lat)
        for d, peer in lat_peers:
            lat_out(i, d, peer).start()
        keep = pltpu.make_async_copy(
            res_lat.at[:, i, me_lat], ret_lat.at[:, me_lat * per_lat + i], own_sem.at[i])
        keep.start()
        owns[i] = keep
    for i in range(parts):
        owns[per_lat + i].wait()
        for d, peer in lon_peers:
            lon_in(i, d, peer).wait_recv()
        attend(in_lon, res_lon, i, same_lon)
        for d, peer in lon_peers:
            lon_out(i, d, peer).start()
        keep = pltpu.make_async_copy(
            res_lon.at[:, i, me_lon], ret_lon.at[:, me_lon, pl.ds(i * SUBROWS, SUBROWS)], own_sem.at[per_lat + i])
        keep.start()
        owns[per_lat + i] = keep

    def add(b, i):
        rows = pl.ds(i * SUBROWS, SUBROWS)
        for o in range(4):
            total = ret_lat[o, b, rows, :].astype(F32) + ret_lon[o, b, rows, :].astype(F32)
            total = total.astype(BF16)
            for r in range(lines):
                outs[o][b, i * lines + r] = total[r * cols:(r + 1) * cols]

    for copy in owns:
        copy.wait()
    for i in range(per_lat):
        for d, peer in lat_peers:
            lat_out(i, d, peer).wait_recv()
    for i in range(parts):
        add(me_lon, i)
        for d, peer in lon_peers:
            lon_out(i, d, peer).wait_recv()
            add(lax.rem(me_lon + n_lon - d, n_lon), i)

    for i in range(per_lat):
        for d, peer in lat_peers:
            lat_in(i, d, peer).wait_send()
            lat_out(i, d, peer).wait_send()
    for i in range(parts):
        for d, peer in lon_peers:
            lon_in(i, d, peer).wait_send()
            lon_out(i, d, peer).wait_send()


def store_kernel(*refs):
    held, outs, sem = refs[:4], refs[4:8], refs[8]
    copies = [pltpu.make_async_copy(held[o], outs[o], sem.at[o]) for o in range(4)]
    for copy in copies:
        copy.start()
    for copy in copies:
        copy.wait()


def by_kernel(n_lat, n_lon, queries, key_vectors, values, upstream):
    batch, rows, cols, feats = queries.shape
    tokens = rows * cols
    per_lat, parts = batch // n_lat, tokens // SUBROWS
    lat_buf = pltpu.VMEM((4, per_lat, n_lat, tokens, feats), BF16)
    lon_buf = pltpu.VMEM((4, parts, n_lon, SUBROWS, feats), BF16)
    back_buf = pltpu.VMEM((4, batch, tokens, feats), BF16)
    lat_sem = pltpu.SemaphoreType.DMA((per_lat, n_lat))
    lon_sem = pltpu.SemaphoreType.DMA((parts, n_lon))
    queries, key_vectors, values, upstream = (
        pltpu.with_memory_space_constraint(item, pltpu.HBM) for item in (queries, key_vectors, values, upstream)
    )
    held = pl.pallas_call(
        functools.partial(kernel, n_lat, n_lon),
        out_shape=(jax.ShapeDtypeStruct(queries.shape, BF16),) * 4,
        in_specs=[pl.BlockSpec(memory_space=pltpu.HBM)] * 4,
        out_specs=(pl.BlockSpec(memory_space=pltpu.VMEM),) * 4,
        scratch_shapes=[
            pltpu.VMEM((4,) + queries.shape, BF16), back_buf,
            lat_buf, lon_buf, lat_buf, lon_buf, back_buf, back_buf,
            lat_sem, lat_sem, lon_sem, lon_sem, lat_sem, lat_sem, lon_sem, lon_sem,
            pltpu.SemaphoreType.DMA((per_lat + parts,)),
            pltpu.SemaphoreType.DMA((4,)),
        ],
        compiler_params=pltpu.CompilerParams(
            collective_id=0, has_side_effects=True, vmem_limit_bytes=40 * 1024 * 1024
        ),
    )(queries, key_vectors, values, upstream)
    return pl.pallas_call(
        store_kernel,
        out_shape=(jax.ShapeDtypeStruct(queries.shape, BF16),) * 4,
        in_specs=[pl.BlockSpec(memory_space=pl.ANY)] * 4,
        out_specs=(pl.BlockSpec(memory_space=pltpu.HBM),) * 4,
        scratch_shapes=[pltpu.SemaphoreType.DMA((4,))],
        compiler_params=pltpu.CompilerParams(vmem_limit_bytes=1024 * 1024),
    )(*held)


def split_heads(tensor):
    leading = tensor.shape[0] * tensor.shape[1]
    return tensor.reshape(leading, tensor.shape[2], tensor.shape[3] // HEAD_DIM, HEAD_DIM)


def lines_whole(items):
    q, k, v, g = (split_heads(item) for item in items)
    dot = functools.partial(jnp.einsum, preferred_element_type=F32)
    probs = jax.nn.softmax(dot("nqhd,nkhd->nhqk", q, k) * SCALE, axis=-1)
    rounded = probs.astype(BF16)
    gprobs = dot("nqhd,nkhd->nhqk", g, v)
    delta = jnp.sum(probs * gprobs, axis=-1, keepdims=True)
    gscores = (probs * (gprobs - delta)).astype(BF16)
    results = (
        dot("nhqk,nkhd->nqhd", rounded, v),
        dot("nhqk,nkhd->nqhd", gscores, k) * SCALE,
        dot("nhqk,nqhd->nkhd", gscores, q) * SCALE,
        dot("nhqk,nqhd->nkhd", rounded, g),
    )
    return tuple(item.astype(BF16).reshape(items[0].shape) for item in results)


def by_exchange(axis, groups, inputs):
    def there(item):
        lines = item.reshape((groups, item.shape[0] * item.shape[1] // groups) + item.shape[2:])
        return lax.all_to_all(lines, axis, split_axis=0, concat_axis=2, tiled=True)

    def back(item):
        item = lax.all_to_all(item, axis, split_axis=2, concat_axis=0, tiled=True)
        return item.reshape(inputs[0].shape)

    return tuple(back(item) for item in lines_whole(tuple(there(item) for item in inputs)))


def by_collectives(n_lat, n_lon, *inputs):
    lon = by_exchange("lon", n_lon, inputs)
    lat = by_exchange("lat", n_lat, tuple(item.transpose(0, 2, 1, 3) for item in inputs))
    return tuple(
        (a.transpose(0, 2, 1, 3).astype(F32) + b.astype(F32)).astype(BF16) for a, b in zip(lat, lon)
    )


def solution(mesh):
    n_lat, n_lon = mesh.shape["lat"], mesh.shape["lon"]

    def on_device(*inputs):
        batch, rows, cols, feats = inputs[0].shape
        fits = (
            batch % n_lat == 0 and batch == n_lon and n_lat > 1 and (rows * cols) % SUBROWS == 0
            and SUBROWS % cols == 0 and feats % LANES == 0 and 2 * HEAD_DIM == LANES
        )
        return (by_kernel if fits else by_collectives)(n_lat, n_lon, *inputs)

    spec = P(None, "lat", "lon", None)
    return jax.shard_map(on_device, mesh=mesh, in_specs=(spec,) * 4, out_specs=(spec,) * 4, check_vma=False)
```

```python
import functools

import jax
import jax.numpy as jnp
from jax import lax
from jax.experimental import pallas as pl
from jax.experimental.pallas import tpu as pltpu
from jax.sharding import PartitionSpec as P

HEAD_DIM = 64
LANES = 128
SUBROWS = 16
SCALE = HEAD_DIM ** (-0.5)
F32 = jnp.float32
BF16 = jnp.bfloat16


def contract(left, right, dims):
    return lax.dot_general(left, right, ((dims[:1], dims[1:]), ((), ())), preferred_element_type=F32)


def lines_block(q, k, v, g, same, low, high):
    tokens = q.shape[0]
    q2 = jnp.concatenate([q * low, q * high], axis=0)
    k2 = jnp.concatenate([k * low, k * high], axis=0)
    v2 = jnp.concatenate([v * low, v * high], axis=0)
    g2 = jnp.concatenate([g * low, g * high], axis=0)
    scores = contract(q, k2, (1, 1))
    gprobs = contract(g, v2, (1, 1))
    probs_b, gscores_b = [], []
    for head in range(2):
        cut = slice(head * tokens, (head + 1) * tokens)
        s = jnp.where(same, scores[:, cut] * SCALE, -1e30)
        e = jnp.exp(s - jnp.max(s, axis=1, keepdims=True))
        p = e / jnp.sum(e, axis=1, keepdims=True)
        d = gprobs[:, cut]
        delta = jnp.sum(p * d, axis=1, keepdims=True)
        probs_b.append(p.astype(BF16))
        gscores_b.append((p * (d - delta)).astype(BF16))
    out = contract(jnp.concatenate(probs_b, axis=1), v2, (1, 0))
    dq = contract(jnp.concatenate(gscores_b, axis=1), k2, (1, 0)) * SCALE
    dk = contract(jnp.concatenate(gscores_b, axis=0), q2, (0, 0)) * SCALE
    dv = contract(jnp.concatenate(probs_b, axis=0), g2, (0, 0))
    return out.astype(BF16), dq.astype(BF16), dk.astype(BF16), dv.astype(BF16)


def kernel(
    n_lat, n_lon, *refs,
):
    given, outs = refs[:4], refs[4:8]
    (
        near, x_ref, in_lat, in_lon, res_lat, res_lon, ret_lat, ret_lon,
    s_in_lat, r_in_lat, s_in_lon, r_in_lon, s_out_lat, r_out_lat, s_out_lon, r_out_lon, own_sem, load_sem,
    ) = refs[8:]
    me_lat = lax.axis_index("lat")
    me_lon = lax.axis_index("lon")
    _, batch, tokens, feats = x_ref.shape
    cols = near.shape[3]
    lines = SUBROWS // cols
    per_lat = batch // n_lat
    parts = tokens // SUBROWS
    lat_peers = [(d, lax.rem(me_lat + d, n_lat)) for d in range(1, n_lat)]
    lon_order = sorted(range(1, n_lon), key=lambda d: (abs(d - n_lon // 2), -d))
    lon_peers = [(d, lax.rem(me_lon + d, n_lon)) for d in lon_order]

    loads = [pltpu.make_async_copy(given[a], near.at[a], load_sem.at[a]) for a in range(4)]
    for copy in loads:
        copy.start()

    barrier = pltpu.get_barrier_semaphore()
    for _, peer in lat_peers:
        pl.semaphore_signal(barrier, inc=1, device_id={"lat": peer}, device_id_type=pl.DeviceIdType.MESH)
    for _, peer in lon_peers:
        pl.semaphore_signal(barrier, inc=1, device_id={"lon": peer}, device_id_type=pl.DeviceIdType.MESH)
    pl.semaphore_wait(barrier, len(lat_peers) + len(lon_peers))

    def remote(src, dst, send, recv, target):
        return pltpu.make_async_remote_copy(
            src_ref=src, dst_ref=dst, send_sem=send, recv_sem=recv,
            device_id=target, device_id_type=pl.DeviceIdType.MESH,
        )

    def lat_in(d, peer):
        return remote(
            x_ref.at[:, pl.ds(peer * per_lat, per_lat)], in_lat.at[:, :, me_lat],
            s_in_lat.at[d], r_in_lat.at[d], {"lat": peer},
        )

    def lon_in(i, d, peer):
        return remote(
            x_ref.at[:, peer, pl.ds(i * SUBROWS, SUBROWS)], in_lon.at[:, i, me_lon],
            s_in_lon.at[i, d], r_in_lon.at[i, d], {"lon": peer},
        )

    def lat_out(d, peer):
        return remote(
            res_lat.at[:, :, peer], ret_lat.at[:, pl.ds(me_lat * per_lat, per_lat)],
            s_out_lat.at[d], r_out_lat.at[d], {"lat": peer},
        )

    def lon_out(i, d, peer):
        return remote(
            res_lon.at[:, i, peer], ret_lon.at[:, me_lon, pl.ds(i * SUBROWS, SUBROWS)],
            s_out_lon.at[i, d], r_out_lon.at[i, d], {"lon": peer},
        )

    def lay(b, i):
        for a in range(4):
            for r in range(lines):
                x_ref[a, b, pl.ds(i * SUBROWS + r * cols, cols), :] = near[a, b, i * lines + r]

    for copy in loads:
        copy.wait()
    for d, peer in lon_peers:
        lay(peer, 0)
        lon_in(0, d, peer).start()
    lay(me_lon, 0)

    def lay_rest(b, carry):
        for i in range(1, parts):
            lay(b, i)
        return carry

    lax.fori_loop(0, batch, lay_rest, 0)
    for d, peer in lat_peers:
        lat_in(d, peer).start()
    for i in range(1, parts):
        for d, peer in lon_peers:
            lon_in(i, d, peer).start()

    owns = []
    for i in range(per_lat):
        owns.append(pltpu.make_async_copy(
            x_ref.at[:, me_lat * per_lat + i], in_lat.at[:, i, me_lat], own_sem.at[len(owns)]))
    for i in range(parts):
        owns.append(pltpu.make_async_copy(
            x_ref.at[:, me_lon, pl.ds(i * SUBROWS, SUBROWS)], in_lon.at[:, i, me_lon], own_sem.at[len(owns)]))
    for copy in owns:
        copy.start()

    lane = lax.broadcasted_iota(jnp.int32, (1, LANES), 1)
    low = (lane < HEAD_DIM).astype(F32).astype(BF16)
    high = (lane >= HEAD_DIM).astype(F32).astype(BF16)

    def attend(arrived, result, i, same):
        count, rows = arrived.shape[2], arrived.shape[3]

        def pair(h, carry):
            cut = pl.ds(pl.multiple_of(h * LANES, LANES), LANES)
            items = [arrived[a, i, :, :, cut].reshape(count * rows, LANES) for a in range(4)]
            for o, value in enumerate(lines_block(*items, same, low, high)):
                result[o, i, :, :, cut] = value.reshape(count, rows, LANES)
            return carry

        lax.fori_loop(0, feats // LANES, pair, 0)

    def same_line(size, line_of):
        a = line_of(lax.broadcasted_iota(jnp.int32, (size, size), 0))
        b = line_of(lax.broadcasted_iota(jnp.int32, (size, size), 1))
        return a == b

    same_lat = same_line(n_lat * tokens, lambda t: lax.rem(t, cols))
    same_lon = same_line(n_lon * SUBROWS, lambda t: lax.div(lax.rem(t, SUBROWS), cols))

    for d, peer in lat_peers:
        lat_in(d, peer).wait_recv()
    for i in range(per_lat):
        owns[i].wait()
        attend(in_lat, res_lat, i, same_lat)
        keep = pltpu.make_async_copy(
            res_lat.at[:, i, me_lat], ret_lat.at[:, me_lat * per_lat + i], own_sem.at[i])
        keep.start()
        owns[i] = keep
    for d, peer in lat_peers:
        lat_out(d, peer).start()
    for i in range(parts):
        owns[per_lat + i].wait()
        for d, peer in lon_peers:
            lon_in(i, d, peer).wait_recv()
        attend(in_lon, res_lon, i, same_lon)
        for d, peer in lon_peers:
            lon_out(i, d, peer).start()
        keep = pltpu.make_async_copy(
            res_lon.at[:, i, me_lon], ret_lon.at[:, me_lon, pl.ds(i * SUBROWS, SUBROWS)], own_sem.at[per_lat + i])
        keep.start()
        owns[per_lat + i] = keep

    def add(b, i):
        rows = pl.ds(i * SUBROWS, SUBROWS)
        for o in range(4):
            total = ret_lat[o, b, rows, :].astype(F32) + ret_lon[o, b, rows, :].astype(F32)
            total = total.astype(BF16)
            for r in range(lines):
                outs[o][b, i * lines + r] = total[r * cols:(r + 1) * cols]

    for copy in owns:
        copy.wait()
    for d, peer in lat_peers:
        lat_out(d, peer).wait_recv()
    for i in range(parts):
        add(me_lon, i)
        for d, peer in lon_peers:
            lon_out(i, d, peer).wait_recv()
            add(lax.rem(me_lon + n_lon - d, n_lon), i)

    for d, peer in lat_peers:
        lat_in(d, peer).wait_send()
        lat_out(d, peer).wait_send()
    for i in range(parts):
        for d, peer in lon_peers:
            lon_in(i, d, peer).wait_send()
            lon_out(i, d, peer).wait_send()


def store_kernel(*refs):
    held, outs, sem = refs[:4], refs[4:8], refs[8]
    copies = [pltpu.make_async_copy(held[o], outs[o], sem.at[o]) for o in range(4)]
    for copy in copies:
        copy.start()
    for copy in copies:
        copy.wait()


def by_kernel(n_lat, n_lon, queries, key_vectors, values, upstream):
    batch, rows, cols, feats = queries.shape
    tokens = rows * cols
    per_lat, parts = batch // n_lat, tokens // SUBROWS
    lat_buf = pltpu.VMEM((4, per_lat, n_lat, tokens, feats), BF16)
    lon_buf = pltpu.VMEM((4, parts, n_lon, SUBROWS, feats), BF16)
    back_buf = pltpu.VMEM((4, batch, tokens, feats), BF16)
    lat_sem = pltpu.SemaphoreType.DMA((n_lat,))
    lon_sem = pltpu.SemaphoreType.DMA((parts, n_lon))
    queries, key_vectors, values, upstream = (
        pltpu.with_memory_space_constraint(item, pltpu.HBM) for item in (queries, key_vectors, values, upstream)
    )
    held = pl.pallas_call(
        functools.partial(kernel, n_lat, n_lon),
        out_shape=(jax.ShapeDtypeStruct(queries.shape, BF16),) * 4,
        in_specs=[pl.BlockSpec(memory_space=pltpu.HBM)] * 4,
        out_specs=(pl.BlockSpec(memory_space=pltpu.VMEM),) * 4,
        scratch_shapes=[
            pltpu.VMEM((4,) + queries.shape, BF16), back_buf,
            lat_buf, lon_buf, lat_buf, lon_buf, back_buf, back_buf,
            lat_sem, lat_sem, lon_sem, lon_sem, lat_sem, lat_sem, lon_sem, lon_sem,
            pltpu.SemaphoreType.DMA((per_lat + parts,)),
            pltpu.SemaphoreType.DMA((4,)),
        ],
        compiler_params=pltpu.CompilerParams(
            collective_id=0, has_side_effects=True, vmem_limit_bytes=40 * 1024 * 1024
        ),
    )(queries, key_vectors, values, upstream)
    return pl.pallas_call(
        store_kernel,
        out_shape=(jax.ShapeDtypeStruct(queries.shape, BF16),) * 4,
        in_specs=[pl.BlockSpec(memory_space=pl.ANY)] * 4,
        out_specs=(pl.BlockSpec(memory_space=pltpu.HBM),) * 4,
        scratch_shapes=[pltpu.SemaphoreType.DMA((4,))],
        compiler_params=pltpu.CompilerParams(vmem_limit_bytes=1024 * 1024),
    )(*held)


def split_heads(tensor):
    leading = tensor.shape[0] * tensor.shape[1]
    return tensor.reshape(leading, tensor.shape[2], tensor.shape[3] // HEAD_DIM, HEAD_DIM)


def lines_whole(items):
    q, k, v, g = (split_heads(item) for item in items)
    dot = functools.partial(jnp.einsum, preferred_element_type=F32)
    probs = jax.nn.softmax(dot("nqhd,nkhd->nhqk", q, k) * SCALE, axis=-1)
    rounded = probs.astype(BF16)
    gprobs = dot("nqhd,nkhd->nhqk", g, v)
    delta = jnp.sum(probs * gprobs, axis=-1, keepdims=True)
    gscores = (probs * (gprobs - delta)).astype(BF16)
    results = (
        dot("nhqk,nkhd->nqhd", rounded, v),
        dot("nhqk,nkhd->nqhd", gscores, k) * SCALE,
        dot("nhqk,nqhd->nkhd", gscores, q) * SCALE,
        dot("nhqk,nqhd->nkhd", rounded, g),
    )
    return tuple(item.astype(BF16).reshape(items[0].shape) for item in results)


def by_exchange(axis, groups, inputs):
    def there(item):
        lines = item.reshape((groups, item.shape[0] * item.shape[1] // groups) + item.shape[2:])
        return lax.all_to_all(lines, axis, split_axis=0, concat_axis=2, tiled=True)

    def back(item):
        item = lax.all_to_all(item, axis, split_axis=2, concat_axis=0, tiled=True)
        return item.reshape(inputs[0].shape)

    return tuple(back(item) for item in lines_whole(tuple(there(item) for item in inputs)))


def by_collectives(n_lat, n_lon, *inputs):
    lon = by_exchange("lon", n_lon, inputs)
    lat = by_exchange("lat", n_lat, tuple(item.transpose(0, 2, 1, 3) for item in inputs))
    return tuple(
        (a.transpose(0, 2, 1, 3).astype(F32) + b.astype(F32)).astype(BF16) for a, b in zip(lat, lon)
    )


def solution(mesh):
    n_lat, n_lon = mesh.shape["lat"], mesh.shape["lon"]

    def on_device(*inputs):
        batch, rows, cols, feats = inputs[0].shape
        fits = (
            batch % n_lat == 0 and batch == n_lon and n_lat > 1 and (rows * cols) % SUBROWS == 0
            and SUBROWS % cols == 0 and feats % LANES == 0 and 2 * HEAD_DIM == LANES
        )
        return (by_kernel if fits else by_collectives)(n_lat, n_lon, *inputs)

    spec = P(None, "lat", "lon", None)
    return jax.shard_map(on_device, mesh=mesh, in_specs=(spec,) * 4, out_specs=(spec,) * 4, check_vma=False)
```
